32 devices in a mesh: runs: 2 (over y), pts: 4 (over z), tm: 2 (over x), rep: 2 (over core).
Axes of the slice: x: 2, y: 2, z: 4, core: 2. Of those that a mesh axis runs over, the one named last changes fastest.
Arguments:
- wind_speed: bfloat16 [256, 1024], P(('runs', 'pts'), 'tm'), parts along dimension 0, may hold values from -6 to 6
- span_of_point: int32 [8192], P('pts'), may hold values from 0 to 127, as said below
- drag_factor: float32 [8192], P('pts'), may hold values from 0.3 to 3
- mode_shapes: bfloat16 [8192, 4096], P('pts', 'rep'), may hold values from -0.09375 to 0.09375
- damping: float32 [4096], P('rep'), as said below
- turning: float32 [4096], P('rep'), may hold values from 0.05 to 2.5
- prior_state: float32 [4, 4096], P('runs', 'rep'), parts along dimension 0, may hold values from -6 to 6
- recovery: bfloat16 [4096, 2048], P('rep', 'pts'), may hold values from -0.125 to 0.125
Outputs:
- stress: bfloat16 [2048, 2048], P(('runs', 'tm'), ('pts', 'rep')), parts along dimension 0
The draws below stay inside these ranges and needn't reach their ends.
There are 2 independent parts, one for each index of `runs`. The reference program is written for one: setup_inputs(seed, part) draws one part's arguments, and reference() takes and returns one part's arrays. A program takes and returns all parts, laid end to end along the dimension named above; an argument that names none is the same for every part. Nothing has to cross between parts.
Inputs may be any that keep to these rules, and one draw needn't show every extreme that they name: `span_of_point`: load points lie in the spans of the same index of pts, 32 spans to an index, and their span never falls along the points. `damping`: every decay rate is positive and at most 1/30.
All inputs are finite; a program needn't handle non-finite values.
Results may differ from the reference program's by a relative error of at most 0.015.
Values may be sent and summed in bfloat16 or wider, within the bound.
A program may use at most 64 MiB of HBM per device.

```python
import math
import jax
import jax.numpy as jnp
from jax import lax

MODES = 4096
PTS_DEV = 2048
SPAN_DEV = 32
WIN = 1024
POINTS = 8192
SPANS = 128
CLAMPS = 2048
N_PTS = 4


def draw_span_of_point(key, part):
    key = jax.random.fold_in(key, 5)
    groups = POINTS // PTS_DEV
    drawn = jax.random.randint(key, (groups, PTS_DEV), 0, SPAN_DEV)
    ordered = jnp.sort(drawn, axis=1)
    ordered = ordered.at[:, 0].set(0).at[:, PTS_DEV - 1].set(SPAN_DEV - 1)
    first_span = jnp.arange(groups, dtype=jnp.int32)[:, None] * SPAN_DEV
    return (ordered + first_span).reshape(POINTS).astype(jnp.int32)


def draw_damping(key, part):
    key = jax.random.fold_in(key, 9)
    pick_key, slow_key, fast_key = jax.random.split(key, 3)
    fast_share = 0.5
    slow_rate = jnp.exp(jax.random.uniform(slow_key, (MODES,), jnp.float32, math.log(0.05 / WIN), math.log(1.5 / WIN)))
    fast_rate = jnp.exp(jax.random.uniform(fast_key, (MODES,), jnp.float32, math.log(1.0 / 50.0), math.log(1.0 / 30.0)))
    chosen = jax.random.uniform(pick_key, (MODES,), jnp.float32) < fast_share
    return jnp.where(chosen, fast_rate, slow_rate).astype(jnp.float32)


def spiked(result, rng, source, target, blocks, factor):
    owner, partner = [(jnp.arange(result.shape[dim]) // (result.shape[dim] // blocks)).reshape([-1 if axis == dim else 1 for axis in range(result.ndim)]) for dim in (source, target)]
    chosen = jax.random.permutation(rng, blocks)[partner]
    strong = (owner == chosen) | (owner == (partner + blocks // 2) % blocks)
    return jnp.where(strong, factor * result, result)


def steps_of(own_key, extent, pieces, smallest, largest):
    loudness, own = 1.0, jax.random.fold_in(own_key, 6)
    for position, blocks in pieces:
        steps = jnp.exp(jax.random.uniform(jax.random.fold_in(own, position), (blocks,), jnp.float32, smallest / len(pieces), largest / len(pieces)))
        loudness = loudness * jnp.repeat(steps, extent[position] // blocks).reshape([-1 if axis == position else 1 for axis in range(len(extent))])
    return loudness


def normal_values(rng, shape, spread, limit, cuts=(), kind=jnp.bfloat16):
    result = spread * jax.random.normal(rng, shape, jnp.float32)
    if cuts:
        result = result * steps_of(rng, shape, cuts, -0.22, 0.18)
    return jnp.clip(result, -limit, limit).astype(kind)


def bell_draw_with(stream_key, extent, width, most, pieces, heavy, held_as=jnp.bfloat16):
    values = width * jax.random.normal(stream_key, extent, jnp.float32)
    if pieces:
        values = values * steps_of(stream_key, extent, pieces, -0.22, 0.18)
    return jnp.clip(spiked(values, jax.random.fold_in(stream_key, 3), *heavy), -most, most).astype(held_as)


def setup_inputs(seed: int = 0, part: int = 0) -> dict:
    keys = jax.random.split(jax.random.key(seed), 9)
    own_keys = jax.random.split(jax.random.fold_in(keys[8], part), 9)
    wind_speed = normal_values(own_keys[0], (SPANS, WIN), 1.0, 6.0, ((0, 4), (1, 2)))
    span_of_point = draw_span_of_point(jax.random.fold_in(keys[8], 71), part)
    drag_factor = jnp.clip(jnp.exp(math.log(3.0) - 2.3025851 * jax.random.uniform(keys[2], (POINTS,), jnp.float32) ** steps_of(keys[2], (POINTS,), ((0, 4),), -0.2, 0.2)), 0.3, 3.0)
    mode_shapes = bell_draw_with(keys[3], (POINTS, MODES), POINTS ** -0.5, 0.09375, ((0, 4), (1, 2)), (0, 1, 4, 2.0))
    damping = draw_damping(jax.random.fold_in(keys[8], 71), part)
    turning = jnp.clip(0.05 + 2.45 * jax.random.uniform(keys[5], (MODES,), jnp.float32) ** steps_of(keys[5], (MODES,), ((0, 2),), -0.2, 0.2), 0.05, 2.5)
    prior_state = normal_values(own_keys[6], (2, MODES), 1.0, 6.0, ((1, 2),), jnp.float32)
    recovery = bell_draw_with(keys[7], (MODES, CLAMPS), MODES ** -0.5, 0.125, ((0, 2), (1, 4)), (0, 1, 4, 2.0))
    return {"wind_speed": wind_speed, "span_of_point": span_of_point, "drag_factor": drag_factor, "mode_shapes": mode_shapes, "damping": damping, "turning": turning, "prior_state": prior_state, "recovery": recovery}


def reference(wind_speed, span_of_point, drag_factor, mode_shapes, damping, turning, prior_state, recovery):
    at_points = wind_speed[span_of_point, :].astype(jnp.float32)
    point_loads = (drag_factor[:, None] * at_points * jnp.abs(at_points)).astype(jnp.bfloat16)

    def add_group(group_index, running):
        first_row = (group_index * PTS_DEV).astype(jnp.int32)
        load_rows = lax.dynamic_slice_in_dim(point_loads, first_row, PTS_DEV, 0)
        shape_rows = lax.dynamic_slice_in_dim(mode_shapes, first_row, PTS_DEV, 0)
        partial_value = lax.dot_general(load_rows, shape_rows, (((0,), (0,)), ((), ())), preferred_element_type=jnp.float32)
        rounded = lax.optimization_barrier(partial_value.astype(jnp.bfloat16))
        return running + rounded.astype(jnp.float32)
    forces = lax.fori_loop(0, N_PTS, add_group, jnp.zeros((WIN, MODES), jnp.float32))
    gain = jnp.sqrt(1.0 - jnp.exp(-2.0 * damping))
    rot_real = jnp.exp(-damping) * jnp.cos(turning)
    rot_imag = jnp.exp(-damping) * jnp.sin(turning)

    def advance(state, driving):
        state_real, state_imag = state
        next_real = rot_real * state_real - rot_imag * state_imag + driving
        next_imag = rot_real * state_imag + rot_imag * state_real
        return ((next_real, next_imag), next_imag)
    _, imaginary = lax.scan(advance, (prior_state[0], prior_state[1]), forces * gain[None, :])
    response = imaginary.astype(jnp.bfloat16)
    return jnp.dot(response, recovery, preferred_element_type=jnp.float32).astype(jnp.bfloat16)
```

```python
import functools

import jax
import jax.numpy as jnp
from jax import lax
from jax.experimental import pallas as pl
from jax.experimental.pallas import tpu as pltpu
from jax.sharding import PartitionSpec as P

CHUNKS = 8
F32 = jnp.float32
BF16 = jnp.bfloat16


def times(a, b):
    return (a[0] * b[0] - a[1] * b[1], a[0] * b[1] + a[1] * b[0])


def power(base, exponent):
    result = None
    while exponent:
        if exponent % 2:
            result = base if result is None else times(result, base)
        exponent //= 2
        if exponent:
            base = times(base, base)
    return result


def remote(src, dst, send_sem, recv_sem, where):
    return pltpu.make_async_remote_copy(
        src_ref=src,
        dst_ref=dst,
        send_sem=send_sem,
        recv_sem=recv_sem,
        device_id=where,
        device_id_type=pl.DeviceIdType.MESH,
    )


def kernel(
    sizes,
    wind_ref, span_ref, drag_ref, shapes_ref, damp_ref, turn_ref, prior_ref, rec_ref,
    out_ref,
    shapes_v, rec_v, winds, bases, forces, ends, entry, coef, resp, part_out, part_in,
    load_sem, wsend, wrecv, zsend, zrecv, xsend, xrecv, esend, erecv, rsend, rrecv,
):
    n_r, n_z, n_t = sizes
    groups = n_r * n_t
    spans, steps = wind_ref.shape
    modes = damp_ref.shape[1]
    width = modes // groups
    length = steps // CHUNKS
    clamps = rec_ref.shape[1]
    half = clamps // 2
    r, z, x, c = (lax.axis_index(a) for a in ("runs", "pts", "tm", "rep"))
    mine = r * n_t + x

    def plane(k, sign=1):
        dr, dx = divmod(k, n_t)
        return lax.rem(r + sign * dr + n_r, n_r), lax.rem(x + sign * dx + n_t, n_t)

    def along_z(o):
        return lax.rem(z + o, n_z)

    barrier = pltpu.get_barrier_semaphore()
    peers = [{"pts": along_z(o)} for o in range(1, n_z)]
    for k in range(1, groups):
        pr, px = plane(k)
        peers.append({"runs": pr, "tm": px})
    peers.append({"rep": 1 - c})
    load_shapes = pltpu.make_async_copy(
        shapes_ref.at[:, pl.ds(pl.multiple_of(mine * width, width), width)], shapes_v, load_sem.at[0]
    )
    load_shapes.start()
    load_rec = pltpu.make_async_copy(rec_ref, rec_v, load_sem.at[1])
    for peer in peers:
        pl.semaphore_signal(barrier, inc=1, device_id=peer, device_id_type=pl.DeviceIdType.MESH)

    span_id = lax.broadcasted_iota(jnp.int32, (spans, span_ref.shape[1]), 0)
    spread = jnp.where(span_id == span_ref[...] - z * spans, drag_ref[...], 0.0)
    spread_hi = spread.astype(BF16)
    spread_lo = (spread - spread_hi.astype(F32)).astype(BF16)
    spread2 = jnp.concatenate([spread_hi, spread_lo], axis=0)
    my_damp = damp_ref[:, pl.ds(pl.multiple_of(mine * width, width), width)]
    gain = jnp.sqrt(1.0 - jnp.exp(-2.0 * my_damp))
    own_rows = pl.ds(pl.multiple_of(z * spans, spans), spans)
    winds[own_rows, :] = wind_ref[...]

    pl.semaphore_wait(barrier, len(peers))
    pending = []
    wind_in = []
    order = sorted(range(1, n_z), key=lambda o: min(o, n_z - o))
    for o in order:
        copy = remote(
            wind_ref, winds.at[own_rows, :], wsend.at[o - 1], wrecv.at[o - 1], {"pts": along_z(o)}
        )
        copy.start()
        pending.append(copy)
        wind_in.append(copy)

    load_shapes.wait()
    load_rec.start()
    base2 = jnp.dot(spread2, shapes_v[...], preferred_element_type=F32)
    base = (base2[:spans] + base2[spans:]) * gain
    bases[mine, own_rows, :] = base.astype(BF16)

    z_in = {}
    for o in order:
        block = bases.at[mine, own_rows, :]
        copy = remote(block, block, zsend.at[o - 1], zrecv.at[o - 1], {"pts": along_z(o)})
        copy.start()
        pending.append(copy)
        z_in[o] = copy

    x_in = {k: [] for k in range(1, groups)}

    def forward(block, piece):
        for k in range(1, groups):
            pr, px = plane(k)
            copy = remote(
                block, block, xsend.at[k - 1, piece], xrecv.at[k - 1, piece], {"runs": pr, "tm": px}
            )
            copy.start()
            pending.append(copy)
            x_in[k].append(copy)

    by_block = n_z <= 4
    if by_block:
        forward(bases.at[mine, own_rows, :], 0)

    for i in range(groups):
        cols = slice(i * width, (i + 1) * width)
        decay = jnp.exp(-damp_ref[:, cols])
        turn = turn_ref[:, cols]
        one = (decay * jnp.cos(turn), decay * jnp.sin(turn))
        chunk = power(one, length)
        block_pow = power(chunk, CHUNKS)
        row = lax.broadcasted_iota(jnp.int32, (CHUNKS, width), 0)
        ahead = (jnp.ones((1, width), F32), jnp.zeros((1, width), F32))
        spread_re = jnp.zeros((CHUNKS, width), F32)
        spread_im = jnp.zeros((CHUNKS, width), F32)
        for s in range(CHUNKS):
            spread_re = jnp.where(row == s, ahead[0], spread_re)
            spread_im = jnp.where(row == s, ahead[1], spread_im)
            ahead = times(ahead, chunk)
        full = jnp.zeros((CHUNKS, width), F32)
        for slot, value in enumerate((*one, *chunk, *block_pow)):
            coef[i, slot] = full + value
        coef[i, 6] = spread_re
        coef[i, 7] = spread_im
    row = lax.broadcasted_iota(jnp.int32, (steps, steps), 0)
    col = lax.broadcasted_iota(jnp.int32, (steps, steps), 1)
    shuffle = (col == (row % CHUNKS) * length + row // CHUNKS).astype(BF16)

    for copy in wind_in:
        copy.wait_recv()
    v = lax.dot_general(shuffle, winds[...], (((1,), (1,)), ((), ())), preferred_element_type=F32)
    q = v * jnp.abs(v)
    q_hi = q.astype(BF16)
    q_lo = (q - q_hi.astype(F32)).astype(BF16)
    q2 = jnp.concatenate([q_hi, q_lo], axis=1)

    for o in order:
        z_in[o].wait_recv()
        if by_block:
            src_rows = pl.ds(pl.multiple_of(lax.rem(z - o + n_z, n_z) * spans, spans), spans)
            forward(bases.at[mine, src_rows, :], o)
    if not by_block:
        forward(bases.at[mine], 0)

    e_in = []
    for k in range(groups):
        pr, px = plane(k, -1)
        group = pr * n_t + px
        if k:
            for copy in x_in[k]:
                copy.wait_recv()
        b = bases[group]
        forces[k] = jnp.dot(q2, jnp.concatenate([b, b], axis=0), preferred_element_type=F32)
        zr, zi = coef[group, 0], coef[group, 1]

        def step(j, state, k=k, zr=zr, zi=zi):
            f = forces[k, pl.ds(pl.multiple_of(j * CHUNKS, CHUNKS), CHUNKS), :]
            return (zr * state[0] - zi * state[1] + f, zr * state[1] + zi * state[0])

        zero = jnp.zeros((CHUNKS, width), F32)
        end_re, end_im = lax.fori_loop(0, length, step, (zero, zero), unroll=8)
        chunk = (coef[group, 2][:1], coef[group, 3][:1])
        row8 = lax.broadcasted_iota(jnp.int32, (CHUNKS, width), 0)
        state = (zero[:1], zero[:1])
        in_re, in_im = zero, zero
        for s in range(CHUNKS):
            if s:
                in_re = jnp.where(row8 == s, state[0], in_re)
                in_im = jnp.where(row8 == s, state[1], in_im)
            moved = times(chunk, state)
            state = (moved[0] + end_re[s : s + 1], moved[1] + end_im[s : s + 1])
        entry[k, 0] = in_re
        entry[k, 1] = in_im
        ends[x, group] = jnp.where(row8 == 0, state[0], state[1])
        arrivals = []
        for dx in range(1, n_t):
            block = ends.at[x, group]
            copy = remote(
                block, block, esend.at[group, dx - 1], erecv.at[group, dx - 1],
                {"tm": lax.rem(x + dx, n_t)},
            )
            copy.start()
            pending.append(copy)
            arrivals.append(copy)
        e_in.append(arrivals)

    for k in range(groups):
        pr, px = plane(k, -1)
        group = pr * n_t + px
        for copy in e_in[k]:
            copy.wait_recv()
        cols = pl.ds(pl.multiple_of(group * width, width), width)
        prior = prior_ref[:, cols]
        state = (prior[:1], prior[1:2])
        block_pow = (coef[group, 4][:1], coef[group, 5][:1])
        for y in range(n_t - 1):
            moved = times(block_pow, state)
            e = ends[y, group]
            state = (
                jnp.where(y < x, moved[0] + e[:1], state[0]),
                jnp.where(y < x, moved[1] + e[1:2], state[1]),
            )
        start = times((coef[group, 6], coef[group, 7]), state)
        start = (start[0] + entry[k, 0], start[1] + entry[k, 1])
        zr, zi = coef[group, 0], coef[group, 1]

        def pair(j, state, k=k, zr=zr, zi=zi, cols=cols):
            imag = []
            f2 = forces[k, pl.ds(pl.multiple_of(j * 2 * CHUNKS, 2 * CHUNKS), 2 * CHUNKS), :]
            for s in range(2):
                f = f2[s * CHUNKS : (s + 1) * CHUNKS]
                state = (zr * state[0] - zi * state[1] + f, zr * state[1] + zi * state[0])
                imag.append(state[1])
            rows = pl.ds(pl.multiple_of(j * 2 * CHUNKS, 2 * CHUNKS), 2 * CHUNKS)
            resp[rows, cols] = jnp.concatenate(imag, axis=0).astype(BF16)
            return state

        lax.fori_loop(0, length // 2, pair, start, unroll=4)

    load_rec.wait()
    theirs = pl.ds(pl.multiple_of((1 - c) * half, half), half)
    ours = pl.ds(pl.multiple_of(c * half, half), half)
    part_out[...] = jnp.dot(resp[...], rec_v[:, theirs], preferred_element_type=F32).astype(BF16)
    swap = remote(part_out, part_in, rsend, rrecv, {"rep": 1 - c})
    swap.start()
    own = jnp.dot(resp[...], rec_v[:, ours], preferred_element_type=F32)
    swap.wait_recv()
    total = (own + part_in[...].astype(F32)).astype(BF16)
    restore = (col == (row % length) * CHUNKS + row // length).astype(BF16)
    out_ref[...] = jnp.dot(restore, total, preferred_element_type=F32).astype(BF16)
    swap.wait_send()
    for copy in pending:
        copy.wait_send()


def local(
    wind_speed, span_of_point, drag_factor, mode_shapes, damping, turning, prior_state, recovery
):
    n_r, n_z, n_t = (lax.axis_size(a) for a in ("runs", "pts", "tm"))
    groups = n_r * n_t
    spans, steps = wind_speed.shape
    points, modes = mode_shapes.shape
    clamps = recovery.shape[1]
    width = modes // groups
    pieces = n_z if n_z <= 4 else 1
    vmem = pl.BlockSpec(memory_space=pltpu.VMEM)
    anywhere = pl.BlockSpec(memory_space=pl.ANY)
    dma = pltpu.SemaphoreType.DMA
    return pl.pallas_call(
        functools.partial(kernel, (n_r, n_z, n_t)),
        out_shape=jax.ShapeDtypeStruct((steps, clamps // 2), BF16),
        in_specs=[vmem, vmem, vmem, anywhere, vmem, vmem, vmem, anywhere],
        out_specs=vmem,
        scratch_shapes=[
            pltpu.VMEM((points, width), BF16),
            pltpu.VMEM((modes, clamps), BF16),
            pltpu.VMEM((n_z * spans, steps), BF16),
            pltpu.VMEM((groups, n_z * spans, width), BF16),
            pltpu.VMEM((groups, steps, width), F32),
            pltpu.VMEM((n_t, groups, CHUNKS, width), F32),
            pltpu.VMEM((groups, 2, CHUNKS, width), F32),
            pltpu.VMEM((groups, 8, CHUNKS, width), F32),
            pltpu.VMEM((steps, modes), BF16),
            pltpu.VMEM((steps, clamps // 2), BF16),
            pltpu.VMEM((steps, clamps // 2), BF16),
            dma((2,)),
            dma((n_z - 1,)),
            dma((n_z - 1,)),
            dma((n_z - 1,)),
            dma((n_z - 1,)),
            dma((groups - 1, pieces)),
            dma((groups - 1, pieces)),
            dma((groups, n_t - 1)),
            dma((groups, n_t - 1)),
            dma,
            dma,
        ],
        compiler_params=pltpu.CompilerParams(
            collective_id=0, has_side_effects=True, vmem_limit_bytes=48 * 1024 * 1024
        ),
    )(
        wind_speed,
        span_of_point.reshape(1, points),
        drag_factor.reshape(1, points),
        mode_shapes,
        damping.reshape(1, modes),
        turning.reshape(1, modes),
        prior_state,
        recovery,
    )


def solution(mesh):
    placed = (
        P(("runs", "pts"), "tm"),
        P("pts"),
        P("pts"),
        P("pts", "rep"),
        P("rep"),
        P("rep"),
        P("runs", "rep"),
        P("rep", "pts"),
    )
    return jax.shard_map(
        local,
        mesh=mesh,
        in_specs=placed,
        out_specs=P(("runs", "tm"), ("pts", "rep")),
        check_vma=False,
    )
```

```python
import functools

import jax
import jax.numpy as jnp
from jax import lax
from jax.experimental import pallas as pl
from jax.experimental.pallas import tpu as pltpu
from jax.sharding import PartitionSpec as P

CHUNKS = 8
F32 = jnp.float32
BF16 = jnp.bfloat16


def times(a, b):
    return (a[0] * b[0] - a[1] * b[1], a[0] * b[1] + a[1] * b[0])


def power(base, exponent):
    result = None
    while exponent:
        if exponent % 2:
            result = base if result is None else times(result, base)
        exponent //= 2
        if exponent:
            base = times(base, base)
    return result


def remote(src, dst, send_sem, recv_sem, where):
    return pltpu.make_async_remote_copy(
        src_ref=src,
        dst_ref=dst,
        send_sem=send_sem,
        recv_sem=recv_sem,
        device_id=where,
        device_id_type=pl.DeviceIdType.MESH,
    )


def kernel(
    sizes,
    wind_h, span_h, drag_h, shapes_ref, damp_h, turn_h, prior_h, rec_ref,
    out_ref,
    wind_ref, span_ref, drag_ref, damp_ref, turn_ref, prior_ref, restore,
    shapes_v, rec_v, winds, bases, forces, ends, entry, coef, resp, part_out, part_in,
    load_sem, wsend, wrecv, zsend, zrecv, xsend, xrecv, esend, erecv, rsend, rrecv,
):
    n_r, n_z, n_t = sizes
    groups = n_r * n_t
    spans, steps = wind_ref.shape
    modes = damp_ref.shape[1]
    width = modes // groups
    length = steps // CHUNKS
    clamps = rec_ref.shape[1]
    half = clamps // 2
    r, z, x, c = (lax.axis_index(a) for a in ("runs", "pts", "tm", "rep"))
    mine = r * n_t + x

    def plane(k, sign=1):
        dr, dx = divmod(k, n_t)
        return lax.rem(r + sign * dr + n_r, n_r), lax.rem(x + sign * dx + n_t, n_t)

    def along_z(o):
        return lax.rem(z + o, n_z)

    barrier = pltpu.get_barrier_semaphore()
    peers = [{"pts": along_z(o)} for o in range(1, n_z)]
    for k in range(1, groups):
        pr, px = plane(k)
        peers.append({"runs": pr, "tm": px})
    peers.append({"rep": 1 - c})
    load_shapes = pltpu.make_async_copy(
        shapes_ref.at[:, pl.ds(pl.multiple_of(mine * width, width), width)], shapes_v, load_sem.at[0]
    )
    small = []
    for i, (src, dst) in enumerate((
        (span_h, span_ref), (drag_h, drag_ref), (damp_h, damp_ref),
        (wind_h, wind_ref), (turn_h, turn_ref), (prior_h, prior_ref),
    )):
        small.append(pltpu.make_async_copy(src, dst, load_sem.at[2 + i]))
        small[-1].start()
    load_shapes.start()
    load_rec = pltpu.make_async_copy(rec_ref, rec_v, load_sem.at[1])
    for peer in peers:
        pl.semaphore_signal(barrier, inc=1, device_id=peer, device_id_type=pl.DeviceIdType.MESH)

    for copy in small[:3]:
        copy.wait()
    span_id = lax.broadcasted_iota(jnp.int32, (spans, span_ref.shape[1]), 0)
    spread = jnp.where(span_id == span_ref[...] - z * spans, drag_ref[...], 0.0)
    spread_hi = spread.astype(BF16)
    spread_lo = (spread - spread_hi.astype(F32)).astype(BF16)
    spread2 = jnp.concatenate([spread_hi, spread_lo], axis=0)
    my_damp = damp_ref[:, pl.ds(pl.multiple_of(mine * width, width), width)]
    gain = jnp.sqrt(1.0 - jnp.exp(-2.0 * my_damp))
    own_rows = pl.ds(pl.multiple_of(z * spans, spans), spans)
    small[3].wait()
    winds[own_rows, :] = wind_ref[...]

    pl.semaphore_wait(barrier, len(peers))
    pending = []
    wind_in = []
    order = sorted(range(1, n_z), key=lambda o: min(o, n_z - o))
    for o in order:
        copy = remote(
            wind_ref, winds.at[own_rows, :], wsend.at[o - 1], wrecv.at[o - 1], {"pts": along_z(o)}
        )
        copy.start()
        pending.append(copy)
        wind_in.append(copy)

    load_shapes.wait()
    load_rec.start()
    base2 = jnp.dot(spread2, shapes_v[...], preferred_element_type=F32)
    base = (base2[:spans] + base2[spans:]) * gain
    bases[mine, own_rows, :] = base.astype(BF16)

    z_in = {}
    for o in order:
        block = bases.at[mine, own_rows, :]
        copy = remote(block, block, zsend.at[o - 1], zrecv.at[o - 1], {"pts": along_z(o)})
        copy.start()
        pending.append(copy)
        z_in[o] = copy

    x_in = {k: [] for k in range(1, groups)}

    def forward(block, piece):
        for k in range(1, groups):
            pr, px = plane(k)
            copy = remote(
                block, block, xsend.at[k - 1, piece], xrecv.at[k - 1, piece], {"runs": pr, "tm": px}
            )
            copy.start()
            pending.append(copy)
            x_in[k].append(copy)

    by_block = n_z <= 4
    if by_block:
        forward(bases.at[mine, own_rows, :], 0)

    small[4].wait()
    small[5].wait()
    for i in range(groups):
        cols = slice(i * width, (i + 1) * width)
        decay = jnp.exp(-damp_ref[:, cols])
        turn = turn_ref[:, cols]
        one = (decay * jnp.cos(turn), decay * jnp.sin(turn))
        chunk = power(one, length)
        block_pow = power(chunk, CHUNKS)
        row = lax.broadcasted_iota(jnp.int32, (CHUNKS, width), 0)
        ahead = (jnp.ones((1, width), F32), jnp.zeros((1, width), F32))
        spread_re = jnp.zeros((CHUNKS, width), F32)
        spread_im = jnp.zeros((CHUNKS, width), F32)
        for s in range(CHUNKS):
            spread_re = jnp.where(row == s, ahead[0], spread_re)
            spread_im = jnp.where(row == s, ahead[1], spread_im)
            ahead = times(ahead, chunk)
        full = jnp.zeros((CHUNKS, width), F32)
        for slot, value in enumerate((*one, *chunk, *block_pow)):
            coef[i, slot] = full + value
        coef[i, 6] = spread_re
        coef[i, 7] = spread_im
    row = lax.broadcasted_iota(jnp.int32, (steps, steps), 0)
    col = lax.broadcasted_iota(jnp.int32, (steps, steps), 1)
    low, shift = CHUNKS - 1, CHUNKS.bit_length() - 1
    shuffle = (col == (row & low) * length + (row >> shift)).astype(BF16)
    restore[...] = (row == (col & low) * length + (col >> shift)).astype(BF16)

    for copy in wind_in:
        copy.wait_recv()
    v = lax.dot_general(shuffle, winds[...], (((1,), (1,)), ((), ())), preferred_element_type=F32)
    q = v * jnp.abs(v)
    q_hi = q.astype(BF16)
    q_lo = (q - q_hi.astype(F32)).astype(BF16)
    q2 = jnp.concatenate([q_hi, q_lo], axis=1)

    for o in order:
        z_in[o].wait_recv()
        if by_block:
            src_rows = pl.ds(pl.multiple_of(lax.rem(z - o + n_z, n_z) * spans, spans), spans)
            forward(bases.at[mine, src_rows, :], o)
    if not by_block:
        forward(bases.at[mine], 0)

    e_in = []
    for k in range(groups):
        pr, px = plane(k, -1)
        group = pr * n_t + px
        if k:
            for copy in x_in[k]:
                copy.wait_recv()
        b = bases[group]
        forces[k] = jnp.dot(q2, jnp.concatenate([b, b], axis=0), preferred_element_type=F32)
        zr, zi = coef[group, 0], coef[group, 1]

        def step(j, state, k=k, zr=zr, zi=zi):
            f = forces[k, pl.ds(pl.multiple_of(j * CHUNKS, CHUNKS), CHUNKS), :]
            return (zr * state[0] - zi * state[1] + f, zr * state[1] + zi * state[0])

        zero = jnp.zeros((CHUNKS, width), F32)
        end_re, end_im = lax.fori_loop(0, length, step, (zero, zero), unroll=8)
        chunk = (coef[group, 2][:1], coef[group, 3][:1])
        row8 = lax.broadcasted_iota(jnp.int32, (CHUNKS, width), 0)
        state = (zero[:1], zero[:1])
        in_re, in_im = zero, zero
        for s in range(CHUNKS):
            if s:
                in_re = jnp.where(row8 == s, state[0], in_re)
                in_im = jnp.where(row8 == s, state[1], in_im)
            moved = times(chunk, state)
            state = (moved[0] + end_re[s : s + 1], moved[1] + end_im[s : s + 1])
        entry[k, 0] = in_re
        entry[k, 1] = in_im
        ends[x, group] = jnp.where(row8 == 0, state[0], state[1])
        arrivals = []
        for dx in range(1, n_t):
            block = ends.at[x, group]
            copy = remote(
                block, block, esend.at[group, dx - 1], erecv.at[group, dx - 1],
                {"tm": lax.rem(x + dx, n_t)},
            )
            copy.start()
            pending.append(copy)
            arrivals.append(copy)
        e_in.append(arrivals)

    for k in range(groups):
        pr, px = plane(k, -1)
        group = pr * n_t + px
        for copy in e_in[k]:
            copy.wait_recv()
        cols = pl.ds(pl.multiple_of(group * width, width), width)
        prior = prior_ref[:, cols]
        state = (prior[:1], prior[1:2])
        block_pow = (coef[group, 4][:1], coef[group, 5][:1])
        for y in range(n_t - 1):
            moved = times(block_pow, state)
            e = ends[y, group]
            state = (
                jnp.where(y < x, moved[0] + e[:1], state[0]),
                jnp.where(y < x, moved[1] + e[1:2], state[1]),
            )
        start = times((coef[group, 6], coef[group, 7]), state)
        start = (start[0] + entry[k, 0], start[1] + entry[k, 1])
        zr, zi = coef[group, 0], coef[group, 1]

        def pair(j, state, k=k, zr=zr, zi=zi, cols=cols):
            imag = []
            f2 = forces[k, pl.ds(pl.multiple_of(j * 2 * CHUNKS, 2 * CHUNKS), 2 * CHUNKS), :]
            for s in range(2):
                f = f2[s * CHUNKS : (s + 1) * CHUNKS]
                state = (zr * state[0] - zi * state[1] + f, zr * state[1] + zi * state[0])
                imag.append(state[1])
            rows = pl.ds(pl.multiple_of(j * 2 * CHUNKS, 2 * CHUNKS), 2 * CHUNKS)
            resp[rows, cols] = jnp.concatenate(imag, axis=0).astype(BF16)
            return state

        lax.fori_loop(0, length // 2, pair, start, unroll=4)

    load_rec.wait()
    theirs = pl.ds(pl.multiple_of((1 - c) * half, half), half)
    ours = pl.ds(pl.multiple_of(c * half, half), half)
    part_out[...] = jnp.dot(resp[...], rec_v[:, theirs], preferred_element_type=F32).astype(BF16)
    swap = remote(part_out, part_in, rsend, rrecv, {"rep": 1 - c})
    swap.start()
    own = jnp.dot(resp[...], rec_v[:, ours], preferred_element_type=F32)
    swap.wait_recv()
    total = (own + part_in[...].astype(F32)).astype(BF16)
    out_ref[...] = jnp.dot(restore[...], total, preferred_element_type=F32).astype(BF16)
    swap.wait_send()
    for copy in pending:
        copy.wait_send()


def local(
    wind_speed, span_of_point, drag_factor, mode_shapes, damping, turning, prior_state, recovery
):
    n_r, n_z, n_t = (lax.axis_size(a) for a in ("runs", "pts", "tm"))
    groups = n_r * n_t
    spans, steps = wind_speed.shape
    points, modes = mode_shapes.shape
    clamps = recovery.shape[1]
    width = modes // groups
    pieces = n_z if n_z <= 4 else 1
    vmem = pl.BlockSpec(memory_space=pltpu.VMEM)
    hbm = pl.BlockSpec(memory_space=pltpu.HBM)
    dma = pltpu.SemaphoreType.DMA
    return pl.pallas_call(
        functools.partial(kernel, (n_r, n_z, n_t)),
        out_shape=jax.ShapeDtypeStruct((steps, clamps // 2), BF16),
        in_specs=[hbm] * 8,
        out_specs=vmem,
        scratch_shapes=[
            pltpu.VMEM((spans, steps), BF16),
            pltpu.VMEM((1, points), jnp.int32),
            pltpu.VMEM((1, points), F32),
            pltpu.VMEM((1, modes), F32),
            pltpu.VMEM((1, modes), F32),
            pltpu.VMEM((2, modes), F32),
            pltpu.VMEM((steps, steps), BF16),
            pltpu.VMEM((points, width), BF16),
            pltpu.VMEM((modes, clamps), BF16),
            pltpu.VMEM((n_z * spans, steps), BF16),
            pltpu.VMEM((groups, n_z * spans, width), BF16),
            pltpu.VMEM((groups, steps, width), F32),
            pltpu.VMEM((n_t, groups, CHUNKS, width), F32),
            pltpu.VMEM((groups, 2, CHUNKS, width), F32),
            pltpu.VMEM((groups, 8, CHUNKS, width), F32),
            pltpu.VMEM((steps, modes), BF16),
            pltpu.VMEM((steps, clamps // 2), BF16),
            pltpu.VMEM((steps, clamps // 2), BF16),
            dma((8,)),
            dma((n_z - 1,)),
            dma((n_z - 1,)),
            dma((n_z - 1,)),
            dma((n_z - 1,)),
            dma((groups - 1, pieces)),
            dma((groups - 1, pieces)),
            dma((groups, n_t - 1)),
            dma((groups, n_t - 1)),
            dma,
            dma,
        ],
        compiler_params=pltpu.CompilerParams(
            collective_id=0, has_side_effects=True, vmem_limit_bytes=64 * 1024 * 1024
        ),
    )(
        wind_speed,
        span_of_point.reshape(1, points),
        drag_factor.reshape(1, points),
        mode_shapes,
        damping.reshape(1, modes),
        turning.reshape(1, modes),
        prior_state,
        recovery,
    )


def solution(mesh):
    placed = (
        P(("runs", "pts"), "tm"),
        P("pts"),
        P("pts"),
        P("pts", "rep"),
        P("rep"),
        P("rep"),
        P("runs", "rep"),
        P("rep", "pts"),
    )
    return jax.shard_map(
        local,
        mesh=mesh,
        in_specs=placed,
        out_specs=P(("runs", "tm"), ("pts", "rep")),
        check_vma=False,
    )
```

```python
import functools

import jax
import jax.numpy as jnp
from jax import lax
from jax.experimental import pallas as pl
from jax.experimental.pallas import tpu as pltpu
from jax.sharding import PartitionSpec as P

CHUNKS = 8
F32 = jnp.float32
BF16 = jnp.bfloat16


def times(a, b):
    return (a[0] * b[0] - a[1] * b[1], a[0] * b[1] + a[1] * b[0])


def power(base, exponent):
    result = None
    while exponent:
        if exponent % 2:
            result = base if result is None else times(result, base)
        exponent //= 2
        if exponent:
            base = times(base, base)
    return result


def remote(src, dst, send_sem, recv_sem, where):
    return pltpu.make_async_remote_copy(
        src_ref=src,
        dst_ref=dst,
        send_sem=send_sem,
        recv_sem=recv_sem,
        device_id=where,
        device_id_type=pl.DeviceIdType.MESH,
    )


def kernel(
    sizes,
    wind_h, span_h, drag_h, shapes_ref, damp_h, turn_h, prior_h, rec_ref,
    out_ref,
    wind_ref, span_ref, drag_ref, damp_ref, turn_ref, prior_ref, restore,
    shapes_v, rec_v, winds, bases, forces, ends, entry, coef, resp, partial, part_out, part_in,
    load_sem, wsend, wrecv, zsend, zrecv, xsend, xrecv, esend, erecv, rsend, rrecv,
):
    n_r, n_z, n_t = sizes
    groups = n_r * n_t
    spans, steps = wind_ref.shape
    modes = damp_ref.shape[1]
    width = modes // groups
    length = steps // CHUNKS
    clamps = rec_ref.shape[1]
    half = clamps // 2
    r, z, x, c = (lax.axis_index(a) for a in ("runs", "pts", "tm", "rep"))
    mine = r * n_t + x

    def plane(k, sign=1):
        dr, dx = divmod(k, n_t)
        return lax.rem(r + sign * dr + n_r, n_r), lax.rem(x + sign * dx + n_t, n_t)

    def along_z(o):
        return lax.rem(z + o, n_z)

    barrier = pltpu.get_barrier_semaphore()
    peers = [{"pts": along_z(o)} for o in range(1, n_z)]
    for k in range(1, groups):
        pr, px = plane(k)
        peers.append({"runs": pr, "tm": px})
    peers.append({"rep": 1 - c})
    load_shapes = pltpu.make_async_copy(
        shapes_ref.at[:, pl.ds(pl.multiple_of(mine * width, width), width)], shapes_v, load_sem.at[0]
    )
    small = []
    for i, (src, dst) in enumerate((
        (span_h, span_ref), (drag_h, drag_ref), (damp_h, damp_ref),
        (wind_h, wind_ref), (turn_h, turn_ref), (prior_h, prior_ref),
    )):
        small.append(pltpu.make_async_copy(src, dst, load_sem.at[2 + i]))
        small[-1].start()
    load_shapes.start()
    load_rec = pltpu.make_async_copy(rec_ref, rec_v, load_sem.at[1])
    for peer in peers:
        pl.semaphore_signal(barrier, inc=1, device_id=peer, device_id_type=pl.DeviceIdType.MESH)

    for copy in small[:3]:
        copy.wait()
    span_id = lax.broadcasted_iota(jnp.int32, (spans, span_ref.shape[1]), 0)
    spread = jnp.where(span_id == span_ref[...] - z * spans, drag_ref[...], 0.0)
    spread_hi = spread.astype(BF16)
    spread_lo = (spread - spread_hi.astype(F32)).astype(BF16)
    spread2 = jnp.concatenate([spread_hi, spread_lo], axis=0)
    my_damp = damp_ref[:, pl.ds(pl.multiple_of(mine * width, width), width)]
    gain = jnp.sqrt(1.0 - jnp.exp(-2.0 * my_damp))
    own_rows = pl.ds(pl.multiple_of(z * spans, spans), spans)
    small[3].wait()
    winds[own_rows, :] = wind_ref[...]

    small[4].wait()
    small[5].wait()
    for i in range(groups):
        cols = slice(i * width, (i + 1) * width)
        decay = jnp.exp(-damp_ref[:, cols])
        turn = turn_ref[:, cols]
        one = (decay * jnp.cos(turn), decay * jnp.sin(turn))
        chunk = power(one, length)
        block_pow = power(chunk, CHUNKS)
        row = lax.broadcasted_iota(jnp.int32, (CHUNKS, width), 0)
        ahead = (jnp.ones((1, width), F32), jnp.zeros((1, width), F32))
        spread_re = jnp.zeros((CHUNKS, width), F32)
        spread_im = jnp.zeros((CHUNKS, width), F32)
        for s in range(CHUNKS):
            spread_re = jnp.where(row == s, ahead[0], spread_re)
            spread_im = jnp.where(row == s, ahead[1], spread_im)
            ahead = times(ahead, chunk)
        full = jnp.zeros((CHUNKS, width), F32)
        for slot, value in enumerate((*one, *chunk, *block_pow)):
            coef[i, slot] = full + value
        coef[i, 6] = spread_re
        coef[i, 7] = spread_im
    row = lax.broadcasted_iota(jnp.int32, (steps, steps), 0)
    col = lax.broadcasted_iota(jnp.int32, (steps, steps), 1)
    low, shift = CHUNKS - 1, CHUNKS.bit_length() - 1
    shuffle = (col == (row & low) * length + (row >> shift)).astype(BF16)
    restore[...] = (row == (col & low) * length + (col >> shift)).astype(BF16)

    load_shapes.wait()
    load_rec.start()
    base2 = jnp.dot(spread2, shapes_v[...], preferred_element_type=F32)
    base = (base2[:spans] + base2[spans:]) * gain
    bases[mine, own_rows, :] = base.astype(BF16)

    pl.semaphore_wait(barrier, len(peers))
    pending = []
    order = sorted(range(1, n_z), key=lambda o: min(o, n_z - o))
    z_in = {}
    for o in order:
        block = bases.at[mine, own_rows, :]
        copy = remote(block, block, zsend.at[o - 1], zrecv.at[o - 1], {"pts": along_z(o)})
        copy.start()
        pending.append(copy)
        z_in[o] = copy

    x_in = {k: [] for k in range(1, groups)}

    def forward(block, piece):
        for k in range(1, groups):
            pr, px = plane(k)
            copy = remote(
                block, block, xsend.at[k - 1, piece], xrecv.at[k - 1, piece], {"runs": pr, "tm": px}
            )
            copy.start()
            pending.append(copy)
            x_in[k].append(copy)

    by_block = n_z <= 4
    if by_block:
        forward(bases.at[mine, own_rows, :], 0)

    wind_in = []
    for o in order:
        copy = remote(
            wind_ref, winds.at[own_rows, :], wsend.at[o - 1], wrecv.at[o - 1], {"pts": along_z(o)}
        )
        copy.start()
        pending.append(copy)
        wind_in.append(copy)

    for o in order:
        z_in[o].wait_recv()
        if by_block:
            src_rows = pl.ds(pl.multiple_of(lax.rem(z - o + n_z, n_z) * spans, spans), spans)
            forward(bases.at[mine, src_rows, :], o)
    if not by_block:
        forward(bases.at[mine], 0)

    for copy in wind_in:
        copy.wait_recv()
    v = lax.dot_general(shuffle, winds[...], (((1,), (1,)), ((), ())), preferred_element_type=F32)
    q = v * jnp.abs(v)
    q_hi = q.astype(BF16)
    q_lo = (q - q_hi.astype(F32)).astype(BF16)
    q2 = jnp.concatenate([q_hi, q_lo], axis=1)

    e_in = []

    def first_pass(k):
        pr, px = plane(k, -1)
        group = pr * n_t + px
        if k:
            for copy in x_in[k]:
                copy.wait_recv()
        b = bases[group]
        forces[k] = jnp.dot(q2, jnp.concatenate([b, b], axis=0), preferred_element_type=F32)
        zr, zi = coef[group, 0], coef[group, 1]

        def step(j, state, k=k, zr=zr, zi=zi):
            f = forces[k, pl.ds(pl.multiple_of(j * CHUNKS, CHUNKS), CHUNKS), :]
            return (zr * state[0] - zi * state[1] + f, zr * state[1] + zi * state[0])

        zero = jnp.zeros((CHUNKS, width), F32)
        end_re, end_im = lax.fori_loop(0, length, step, (zero, zero), unroll=8)
        chunk = (coef[group, 2][:1], coef[group, 3][:1])
        row8 = lax.broadcasted_iota(jnp.int32, (CHUNKS, width), 0)
        state = (zero[:1], zero[:1])
        in_re, in_im = zero, zero
        for s in range(CHUNKS):
            if s:
                in_re = jnp.where(row8 == s, state[0], in_re)
                in_im = jnp.where(row8 == s, state[1], in_im)
            moved = times(chunk, state)
            state = (moved[0] + end_re[s : s + 1], moved[1] + end_im[s : s + 1])
        entry[k, 0] = in_re
        entry[k, 1] = in_im
        ends[x, group] = jnp.where(row8 == 0, state[0], state[1])
        arrivals = []
        for dx in range(1, n_t):
            block = ends.at[x, group]
            copy = remote(
                block, block, esend.at[group, dx - 1], erecv.at[group, dx - 1],
                {"tm": lax.rem(x + dx, n_t)},
            )
            copy.start()
            pending.append(copy)
            arrivals.append(copy)
        e_in.append(arrivals)

    def second_pass(k):
        pr, px = plane(k, -1)
        group = pr * n_t + px
        for copy in e_in[k]:
            copy.wait_recv()
        cols = pl.ds(pl.multiple_of(group * width, width), width)
        prior = prior_ref[:, cols]
        state = (prior[:1], prior[1:2])
        block_pow = (coef[group, 4][:1], coef[group, 5][:1])
        for y in range(n_t - 1):
            moved = times(block_pow, state)
            e = ends[y, group]
            state = (
                jnp.where(y < x, moved[0] + e[:1], state[0]),
                jnp.where(y < x, moved[1] + e[1:2], state[1]),
            )
        start = times((coef[group, 6], coef[group, 7]), state)
        start = (start[0] + entry[k, 0], start[1] + entry[k, 1])
        zr, zi = coef[group, 0], coef[group, 1]

        def pair(j, state, k=k, zr=zr, zi=zi, cols=cols):
            imag = []
            f2 = forces[k, pl.ds(pl.multiple_of(j * 2 * CHUNKS, 2 * CHUNKS), 2 * CHUNKS), :]
            for s in range(2):
                f = f2[s * CHUNKS : (s + 1) * CHUNKS]
                state = (zr * state[0] - zi * state[1] + f, zr * state[1] + zi * state[0])
                imag.append(state[1])
            rows = pl.ds(pl.multiple_of(j * 2 * CHUNKS, 2 * CHUNKS), 2 * CHUNKS)
            resp[rows, cols] = jnp.concatenate(imag, axis=0).astype(BF16)
            return state

        lax.fori_loop(0, length // 2, pair, start, unroll=4)
        return cols

    theirs = pl.ds(pl.multiple_of((1 - c) * half, half), half)
    ours = pl.ds(pl.multiple_of(c * half, half), half)
    ahead = 0
    for k in range(groups):
        due = min(groups, max(k + 2, (k // n_t + 1) * n_t))
        for j in range(ahead, due):
            first_pass(j)
        ahead = due
        if k == groups - 1:
            break
        cols = second_pass(k)
        if k == 0:
            load_rec.wait()
        product = jnp.dot(resp[:, cols], rec_v[cols, :], preferred_element_type=F32)
        if k:
            partial[...] += product
        else:
            partial[...] = product
    cols = second_pass(groups - 1)
    last = jnp.dot(resp[:, cols], rec_v[cols, theirs], preferred_element_type=F32)
    part_out[...] = (partial[:, theirs] + last).astype(BF16)
    swap = remote(part_out, part_in, rsend, rrecv, {"rep": 1 - c})
    swap.start()
    last = jnp.dot(resp[:, cols], rec_v[cols, ours], preferred_element_type=F32)
    own = partial[:, ours] + last
    swap.wait_recv()
    total = (own + part_in[...].astype(F32)).astype(BF16)
    out_ref[...] = jnp.dot(restore[...], total, preferred_element_type=F32).astype(BF16)
    swap.wait_send()
    for copy in pending:
        copy.wait_send()


def local(
    wind_speed, span_of_point, drag_factor, mode_shapes, damping, turning, prior_state, recovery
):
    n_r, n_z, n_t = (lax.axis_size(a) for a in ("runs", "pts", "tm"))
    groups = n_r * n_t
    spans, steps = wind_speed.shape
    points, modes = mode_shapes.shape
    clamps = recovery.shape[1]
    width = modes // groups
    pieces = n_z if n_z <= 4 else 1
    vmem = pl.BlockSpec(memory_space=pltpu.VMEM)
    hbm = pl.BlockSpec(memory_space=pltpu.HBM)
    dma = pltpu.SemaphoreType.DMA
    return pl.pallas_call(
        functools.partial(kernel, (n_r, n_z, n_t)),
        out_shape=jax.ShapeDtypeStruct((steps, clamps // 2), BF16),
        in_specs=[hbm] * 8,
        out_specs=vmem,
        scratch_shapes=[
            pltpu.VMEM((spans, steps), BF16),
            pltpu.VMEM((1, points), jnp.int32),
            pltpu.VMEM((1, points), F32),
            pltpu.VMEM((1, modes), F32),
            pltpu.VMEM((1, modes), F32),
            pltpu.VMEM((2, modes), F32),
            pltpu.VMEM((steps, steps), BF16),
            pltpu.VMEM((points, width), BF16),
            pltpu.VMEM((modes, clamps), BF16),
            pltpu.VMEM((n_z * spans, steps), BF16),
            pltpu.VMEM((groups, n_z * spans, width), BF16),
            pltpu.VMEM((groups, steps, width), F32),
            pltpu.VMEM((n_t, groups, CHUNKS, width), F32),
            pltpu.VMEM((groups, 2, CHUNKS, width), F32),
            pltpu.VMEM((groups, 8, CHUNKS, width), F32),
            pltpu.VMEM((steps, modes), BF16),
            pltpu.VMEM((steps, clamps), F32),
            pltpu.VMEM((steps, clamps // 2), BF16),
            pltpu.VMEM((steps, clamps // 2), BF16),
            dma((8,)),
            dma((n_z - 1,)),
            dma((n_z - 1,)),
            dma((n_z - 1,)),
            dma((n_z - 1,)),
            dma((groups - 1, pieces)),
            dma((groups - 1, pieces)),
            dma((groups, n_t - 1)),
            dma((groups, n_t - 1)),
            dma,
            dma,
        ],
        compiler_params=pltpu.CompilerParams(
            collective_id=0, has_side_effects=True, vmem_limit_bytes=64 * 1024 * 1024
        ),
    )(
        wind_speed,
        span_of_point.reshape(1, points),
        drag_factor.reshape(1, points),
        mode_shapes,
        damping.reshape(1, modes),
        turning.reshape(1, modes),
        prior_state,
        recovery,
    )


def solution(mesh):
    placed = (
        P(("runs", "pts"), "tm"),
        P("pts"),
        P("pts"),
        P("pts", "rep"),
        P("rep"),
        P("rep"),
        P("runs", "rep"),
        P("rep", "pts"),
    )
    return jax.shard_map(
        local,
        mesh=mesh,
        in_specs=placed,
        out_specs=P(("runs", "tm"), ("pts", "rep")),
        check_vma=False,
    )
```

```python
import functools

import jax
import jax.numpy as jnp
from jax import lax
from jax.experimental import pallas as pl
from jax.experimental.pallas import tpu as pltpu
from jax.sharding import PartitionSpec as P

CHUNKS = 8
F32 = jnp.float32
BF16 = jnp.bfloat16


def times(a, b):
    return (a[0] * b[0] - a[1] * b[1], a[0] * b[1] + a[1] * b[0])


def power(base, exponent):
    result = None
    while exponent:
        if exponent % 2:
            result = base if result is None else times(result, base)
        exponent //= 2
        if exponent:
            base = times(base, base)
    return result


def remote(src, dst, send_sem, recv_sem, where):
    return pltpu.make_async_remote_copy(
        src_ref=src,
        dst_ref=dst,
        send_sem=send_sem,
        recv_sem=recv_sem,
        device_id=where,
        device_id_type=pl.DeviceIdType.MESH,
    )


def kernel(
    sizes,
    wind_h, span_h, drag_h, shapes_ref, damp_h, turn_h, prior_h, rec_ref,
    out_ref,
    wind_ref, span_ref, drag_ref, damp_ref, turn_ref, prior_ref, restore,
    shapes_v, rec_v, winds, bases, forces, ends, entry, coef, resp, partial, part_out, part_in,
    load_sem, wsend, wrecv, zsend, zrecv, xsend, xrecv, esend, erecv, rsend, rrecv,
):
    n_r, n_z, n_t = sizes
    groups = n_r * n_t
    spans, steps = wind_ref.shape
    modes = damp_ref.shape[1]
    width = modes // groups
    length = steps // CHUNKS
    clamps = rec_ref.shape[1]
    half = clamps // 2
    r, z, x, c = (lax.axis_index(a) for a in ("runs", "pts", "tm", "rep"))
    mine = r * n_t + x

    def plane(k, sign=1):
        dr, dx = divmod(k, n_t)
        return lax.rem(r + sign * dr + n_r, n_r), lax.rem(x + sign * dx + n_t, n_t)

    def along_z(o):
        return lax.rem(z + o, n_z)

    barrier = pltpu.get_barrier_semaphore()
    peers = [{"pts": along_z(o)} for o in range(1, n_z)]
    for k in range(1, groups):
        pr, px = plane(k)
        peers.append({"runs": pr, "tm": px})
    peers.append({"rep": 1 - c})
    load_shapes = pltpu.make_async_copy(
        shapes_ref.at[:, pl.ds(pl.multiple_of(mine * width, width), width)], shapes_v, load_sem.at[0]
    )
    small = []
    for i, (src, dst) in enumerate((
        (span_h, span_ref), (drag_h, drag_ref), (damp_h, damp_ref),
        (wind_h, wind_ref), (turn_h, turn_ref), (prior_h, prior_ref),
    )):
        small.append(pltpu.make_async_copy(src, dst, load_sem.at[2 + i]))
        small[-1].start()
    load_shapes.start()
    load_rec = pltpu.make_async_copy(rec_ref, rec_v, load_sem.at[1])
    for peer in peers:
        pl.semaphore_signal(barrier, inc=1, device_id=peer, device_id_type=pl.DeviceIdType.MESH)

    for copy in small[:3]:
        copy.wait()
    span_id = lax.broadcasted_iota(jnp.int32, (spans, span_ref.shape[1]), 0)
    spread = jnp.where(span_id == span_ref[...] - z * spans, drag_ref[...], 0.0)
    spread_hi = spread.astype(BF16)
    spread_lo = (spread - spread_hi.astype(F32)).astype(BF16)
    spread2 = jnp.concatenate([spread_hi, spread_lo], axis=0)
    my_damp = damp_ref[:, pl.ds(pl.multiple_of(mine * width, width), width)]
    gain = jnp.sqrt(1.0 - jnp.exp(-2.0 * my_damp))
    own_rows = pl.ds(pl.multiple_of(z * spans, spans), spans)
    small[3].wait()
    winds[own_rows, :] = wind_ref[...]

    load_shapes.wait()
    load_rec.start()
    base2 = jnp.dot(spread2, shapes_v[...], preferred_element_type=F32)
    base = (base2[:spans] + base2[spans:]) * gain
    bases[mine, own_rows, :] = base.astype(BF16)

    pl.semaphore_wait(barrier, len(peers))
    pending = []
    order = sorted(range(1, n_z), key=lambda o: min(o, n_z - o))
    z_in = {}
    for o in order:
        block = bases.at[mine, own_rows, :]
        copy = remote(block, block, zsend.at[o - 1], zrecv.at[o - 1], {"pts": along_z(o)})
        copy.start()
        pending.append(copy)
        z_in[o] = copy

    x_in = {k: [] for k in range(1, groups)}

    def forward(block, piece):
        for k in range(1, groups):
            pr, px = plane(k)
            copy = remote(
                block, block, xsend.at[k - 1, piece], xrecv.at[k - 1, piece], {"runs": pr, "tm": px}
            )
            copy.start()
            pending.append(copy)
            x_in[k].append(copy)

    by_block = n_z <= 4
    if by_block:
        forward(bases.at[mine, own_rows, :], 0)

    wind_in = []
    for o in order:
        copy = remote(
            wind_ref, winds.at[own_rows, :], wsend.at[o - 1], wrecv.at[o - 1], {"pts": along_z(o)}
        )
        copy.start()
        pending.append(copy)
        wind_in.append(copy)

    for o in order:
        z_in[o].wait_recv()
        if by_block:
            src_rows = pl.ds(pl.multiple_of(lax.rem(z - o + n_z, n_z) * spans, spans), spans)
            forward(bases.at[mine, src_rows, :], o)
    if not by_block:
        forward(bases.at[mine], 0)

    small[4].wait()
    small[5].wait()
    for i in range(groups):
        cols = slice(i * width, (i + 1) * width)
        decay = jnp.exp(-damp_ref[:, cols])
        turn = turn_ref[:, cols]
        one = (decay * jnp.cos(turn), decay * jnp.sin(turn))
        chunk = power(one, length)
        block_pow = power(chunk, CHUNKS)
        row = lax.broadcasted_iota(jnp.int32, (CHUNKS, width), 0)
        ahead = (jnp.ones((1, width), F32), jnp.zeros((1, width), F32))
        spread_re = jnp.zeros((CHUNKS, width), F32)
        spread_im = jnp.zeros((CHUNKS, width), F32)
        for s in range(CHUNKS):
            spread_re = jnp.where(row == s, ahead[0], spread_re)
            spread_im = jnp.where(row == s, ahead[1], spread_im)
            ahead = times(ahead, chunk)
        full = jnp.zeros((CHUNKS, width), F32)
        for slot, value in enumerate((*one, *chunk, *block_pow)):
            coef[i, slot] = full + value
        coef[i, 6] = spread_re
        coef[i, 7] = spread_im
    row = lax.broadcasted_iota(jnp.int32, (steps, steps), 0)
    col = lax.broadcasted_iota(jnp.int32, (steps, steps), 1)
    low, shift = CHUNKS - 1, CHUNKS.bit_length() - 1
    shuffle = (col == (row & low) * length + (row >> shift)).astype(BF16)
    restore[...] = (row == (col & low) * length + (col >> shift)).astype(BF16)

    for copy in wind_in:
        copy.wait_recv()
    v = lax.dot_general(shuffle, winds[...], (((1,), (1,)), ((), ())), preferred_element_type=F32)
    q = v * jnp.abs(v)
    q_hi = q.astype(BF16)
    q_lo = (q - q_hi.astype(F32)).astype(BF16)
    q2 = jnp.concatenate([q_hi, q_lo], axis=1)

    e_in = []
    sent_ends = []

    def first_pass(k):
        pr, px = plane(k, -1)
        group = pr * n_t + px
        if k:
            for copy in x_in[k]:
                copy.wait_recv()
        b = bases[group]
        forces[k] = jnp.dot(q2, jnp.concatenate([b, b], axis=0), preferred_element_type=F32)
        zr, zi = coef[group, 0], coef[group, 1]

        def step(j, state, k=k, zr=zr, zi=zi):
            f = forces[k, pl.ds(pl.multiple_of(j * CHUNKS, CHUNKS), CHUNKS), :]
            return (zr * state[0] - zi * state[1] + f, zr * state[1] + zi * state[0])

        zero = jnp.zeros((CHUNKS, width), F32)
        end_re, end_im = lax.fori_loop(0, length, step, (zero, zero), unroll=8)
        chunk = (coef[group, 2][:1], coef[group, 3][:1])
        row8 = lax.broadcasted_iota(jnp.int32, (CHUNKS, width), 0)
        state = (zero[:1], zero[:1])
        in_re, in_im = zero, zero
        for s in range(CHUNKS):
            if s:
                in_re = jnp.where(row8 == s, state[0], in_re)
                in_im = jnp.where(row8 == s, state[1], in_im)
            moved = times(chunk, state)
            state = (moved[0] + end_re[s : s + 1], moved[1] + end_im[s : s + 1])
        entry[k, 0] = in_re
        entry[k, 1] = in_im
        ends[x, group] = jnp.where(row8 == 0, state[0], state[1])
        arrivals = []
        for dx in range(1, n_t):
            block = ends.at[x, group]
            copy = remote(
                block, block, esend.at[group, dx - 1], erecv.at[group, dx - 1],
                {"tm": lax.rem(x + dx, n_t)},
            )
            pl.when(x + dx < n_t)(copy.start)
            sent_ends.append((dx, copy))
            arrivals.append((dx, copy))
        e_in.append(arrivals)

    def second_pass(k):
        pr, px = plane(k, -1)
        group = pr * n_t + px
        for dx, copy in e_in[k]:
            pl.when(x >= dx)(copy.wait_recv)
        cols = pl.ds(pl.multiple_of(group * width, width), width)
        prior = prior_ref[:, cols]
        state = (prior[:1], prior[1:2])
        block_pow = (coef[group, 4][:1], coef[group, 5][:1])
        for y in range(n_t - 1):
            moved = times(block_pow, state)
            e = ends[y, group]
            state = (
                jnp.where(y < x, moved[0] + e[:1], state[0]),
                jnp.where(y < x, moved[1] + e[1:2], state[1]),
            )
        start = times((coef[group, 6], coef[group, 7]), state)
        start = (start[0] + entry[k, 0], start[1] + entry[k, 1])
        zr, zi = coef[group, 0], coef[group, 1]

        def pair(j, state, k=k, zr=zr, zi=zi, cols=cols):
            imag = []
            f2 = forces[k, pl.ds(pl.multiple_of(j * 2 * CHUNKS, 2 * CHUNKS), 2 * CHUNKS), :]
            for s in range(2):
                f = f2[s * CHUNKS : (s + 1) * CHUNKS]
                state = (zr * state[0] - zi * state[1] + f, zr * state[1] + zi * state[0])
                imag.append(state[1])
            rows = pl.ds(pl.multiple_of(j * 2 * CHUNKS, 2 * CHUNKS), 2 * CHUNKS)
            resp[rows, cols] = jnp.concatenate(imag, axis=0).astype(BF16)
            return state

        lax.fori_loop(0, length // 2, pair, start, unroll=4)
        return cols

    theirs = pl.ds(pl.multiple_of((1 - c) * half, half), half)
    ours = pl.ds(pl.multiple_of(c * half, half), half)
    for k in range(groups):
        first_pass(k)
    load_rec.wait()
    turns = list(range(groups))
    for i, k in enumerate(turns[:-1]):
        cols = second_pass(k)
        product = jnp.dot(resp[:, cols], rec_v[cols, :], preferred_element_type=F32)
        if i:
            partial[...] += product
        else:
            partial[...] = product
    cols = second_pass(turns[-1])
    last = jnp.dot(resp[:, cols], rec_v[cols, theirs], preferred_element_type=F32)
    part_out[...] = (partial[:, theirs] + last).astype(BF16)
    swap = remote(part_out, part_in, rsend, rrecv, {"rep": 1 - c})
    swap.start()
    last = jnp.dot(resp[:, cols], rec_v[cols, ours], preferred_element_type=F32)
    own = partial[:, ours] + last
    swap.wait_recv()
    total = (own + part_in[...].astype(F32)).astype(BF16)
    out_ref[...] = jnp.dot(restore[...], total, preferred_element_type=F32).astype(BF16)
    swap.wait_send()
    for copy in pending:
        copy.wait_send()
    for dx, copy in sent_ends:
        pl.when(x + dx < n_t)(copy.wait_send)


def local(
    wind_speed, span_of_point, drag_factor, mode_shapes, damping, turning, prior_state, recovery
):
    n_r, n_z, n_t = (lax.axis_size(a) for a in ("runs", "pts", "tm"))
    groups = n_r * n_t
    spans, steps = wind_speed.shape
    points, modes = mode_shapes.shape
    clamps = recovery.shape[1]
    width = modes // groups
    pieces = n_z if n_z <= 4 else 1
    vmem = pl.BlockSpec(memory_space=pltpu.VMEM)
    hbm = pl.BlockSpec(memory_space=pltpu.HBM)
    dma = pltpu.SemaphoreType.DMA
    return pl.pallas_call(
        functools.partial(kernel, (n_r, n_z, n_t)),
        out_shape=jax.ShapeDtypeStruct((steps, clamps // 2), BF16),
        in_specs=[hbm] * 8,
        out_specs=vmem,
        scratch_shapes=[
            pltpu.VMEM((spans, steps), BF16),
            pltpu.VMEM((1, points), jnp.int32),
            pltpu.VMEM((1, points), F32),
            pltpu.VMEM((1, modes), F32),
            pltpu.VMEM((1, modes), F32),
            pltpu.VMEM((2, modes), F32),
            pltpu.VMEM((steps, steps), BF16),
            pltpu.VMEM((points, width), BF16),
            pltpu.VMEM((modes, clamps), BF16),
            pltpu.VMEM((n_z * spans, steps), BF16),
            pltpu.VMEM((groups, n_z * spans, width), BF16),
            pltpu.VMEM((groups, steps, width), F32),
            pltpu.VMEM((n_t, groups, CHUNKS, width), F32),
            pltpu.VMEM((groups, 2, CHUNKS, width), F32),
            pltpu.VMEM((groups, 8, CHUNKS, width), F32),
            pltpu.VMEM((steps, modes), BF16),
            pltpu.VMEM((steps, clamps), F32),
            pltpu.VMEM((steps, clamps // 2), BF16),
            pltpu.VMEM((steps, clamps // 2), BF16),
            dma((8,)),
            dma((n_z - 1,)),
            dma((n_z - 1,)),
            dma((n_z - 1,)),
            dma((n_z - 1,)),
            dma((groups - 1, pieces)),
            dma((groups - 1, pieces)),
            dma((groups, n_t - 1)),
            dma((groups, n_t - 1)),
            dma,
            dma,
        ],
        compiler_params=pltpu.CompilerParams(
            collective_id=0, has_side_effects=True, vmem_limit_bytes=64 * 1024 * 1024
        ),
    )(
        wind_speed,
        span_of_point.reshape(1, points),
        drag_factor.reshape(1, points),
        mode_shapes,
        damping.reshape(1, modes),
        turning.reshape(1, modes),
        prior_state,
        recovery,
    )


def solution(mesh):
    placed = (
        P(("runs", "pts"), "tm"),
        P("pts"),
        P("pts"),
        P("pts", "rep"),
        P("rep"),
        P("rep"),
        P("runs", "rep"),
        P("rep", "pts"),
    )
    return jax.shard_map(
        local,
        mesh=mesh,
        in_specs=placed,
        out_specs=P(("runs", "tm"), ("pts", "rep")),
        check_vma=False,
    )
```

```python
import functools

import jax
import jax.numpy as jnp
from jax import lax
from jax.experimental import pallas as pl
from jax.experimental.pallas import tpu as pltpu
from jax.sharding import PartitionSpec as P

CHUNKS = 8
F32 = jnp.float32
BF16 = jnp.bfloat16


def times(a, b):
    return (a[0] * b[0] - a[1] * b[1], a[0] * b[1] + a[1] * b[0])


def power(base, exponent):
    result = None
    while exponent:
        if exponent % 2:
            result = base if result is None else times(result, base)
        exponent //= 2
        if exponent:
            base = times(base, base)
    return result


def remote(src, dst, send_sem, recv_sem, where):
    return pltpu.make_async_remote_copy(
        src_ref=src,
        dst_ref=dst,
        send_sem=send_sem,
        recv_sem=recv_sem,
        device_id=where,
        device_id_type=pl.DeviceIdType.MESH,
    )


def kernel(
    sizes,
    wind_h, span_h, drag_h, shapes_ref, damp_h, turn_h, prior_h, rec_ref,
    out_ref,
    wind_ref, span_ref, drag_ref, damp_ref, turn_ref, prior_ref, restore,
    shapes_v, rec_v, winds, bases, forces, ends, entry, coef, resp, partial, part_out, part_in,
    load_sem, wsend, wrecv, zsend, zrecv, xsend, xrecv, esend, erecv, rsend, rrecv,
):
    n_r, n_z, n_t = sizes
    groups = n_r * n_t
    spans, steps = wind_ref.shape
    modes = damp_ref.shape[1]
    width = modes // groups
    length = steps // CHUNKS
    clamps = rec_ref.shape[1]
    half = clamps // 2
    r, z, x, c = (lax.axis_index(a) for a in ("runs", "pts", "tm", "rep"))
    mine = r * n_t + x

    def plane(k, sign=1):
        dr, dx = divmod(k, n_t)
        return lax.rem(r + sign * dr + n_r, n_r), lax.rem(x + sign * dx + n_t, n_t)

    def along_z(o):
        return lax.rem(z + o, n_z)

    barrier = pltpu.get_barrier_semaphore()
    peers = [{"pts": along_z(o)} for o in range(1, n_z)]
    for k in range(1, groups):
        pr, px = plane(k)
        peers.append({"runs": pr, "tm": px})
    peers.append({"rep": 1 - c})
    load_shapes = pltpu.make_async_copy(
        shapes_ref.at[:, pl.ds(pl.multiple_of(mine * width, width), width)], shapes_v, load_sem.at[0]
    )
    load_shapes.start()
    small = []
    for i, (src, dst) in enumerate((
        (span_h, span_ref), (drag_h, drag_ref), (damp_h, damp_ref),
        (wind_h, wind_ref), (turn_h, turn_ref), (prior_h, prior_ref),
    )):
        small.append(pltpu.make_async_copy(src, dst, load_sem.at[2 + i]))
        small[-1].start()
    load_rec = pltpu.make_async_copy(rec_ref, rec_v, load_sem.at[1])
    for peer in peers:
        pl.semaphore_signal(barrier, inc=1, device_id=peer, device_id_type=pl.DeviceIdType.MESH)

    for copy in small[:3]:
        copy.wait()
    span_id = lax.broadcasted_iota(jnp.int32, (spans, span_ref.shape[1]), 0)
    spread = jnp.where(span_id == span_ref[...] - z * spans, drag_ref[...], 0.0)
    spread_hi = spread.astype(BF16)
    spread_lo = (spread - spread_hi.astype(F32)).astype(BF16)
    spread2 = jnp.concatenate([spread_hi, spread_lo], axis=0)
    my_damp = damp_ref[:, pl.ds(pl.multiple_of(mine * width, width), width)]
    gain = jnp.sqrt(1.0 - jnp.exp(-2.0 * my_damp))
    own_rows = pl.ds(pl.multiple_of(z * spans, spans), spans)
    small[3].wait()
    winds[own_rows, :] = wind_ref[...]

    load_shapes.wait()
    load_rec.start()
    base2 = jnp.dot(spread2, shapes_v[...], preferred_element_type=F32)
    base = (base2[:spans] + base2[spans:]) * gain
    bases[mine, own_rows, :] = base.astype(BF16)

    pl.semaphore_wait(barrier, len(peers))
    pending = []
    order = sorted(range(1, n_z), key=lambda o: min(o, n_z - o))
    z_in = {}
    for o in order:
        block = bases.at[mine, own_rows, :]
        copy = remote(block, block, zsend.at[o - 1], zrecv.at[o - 1], {"pts": along_z(o)})
        copy.start()
        pending.append(copy)
        z_in[o] = copy

    wind_in = []
    for o in order:
        copy = remote(
            wind_ref, winds.at[own_rows, :], wsend.at[o - 1], wrecv.at[o - 1], {"pts": along_z(o)}
        )
        copy.start()
        pending.append(copy)
        wind_in.append(copy)

    x_in = {k: [] for k in range(1, groups)}

    def forward(block, piece):
        for k in range(1, groups):
            pr, px = plane(k)
            copy = remote(
                block, block, xsend.at[k - 1, piece], xrecv.at[k - 1, piece], {"runs": pr, "tm": px}
            )
            copy.start()
            pending.append(copy)
            x_in[k].append(copy)

    by_block = n_z <= 4
    if by_block:
        forward(bases.at[mine, own_rows, :], 0)

    for o in order:
        z_in[o].wait_recv()
        if by_block:
            src_rows = pl.ds(pl.multiple_of(lax.rem(z - o + n_z, n_z) * spans, spans), spans)
            forward(bases.at[mine, src_rows, :], o)
    if not by_block:
        forward(bases.at[mine], 0)

    small[4].wait()
    small[5].wait()
    for i in range(groups):
        cols = slice(i * width, (i + 1) * width)
        decay = jnp.exp(-damp_ref[:, cols])
        turn = turn_ref[:, cols]
        one = (decay * jnp.cos(turn), decay * jnp.sin(turn))
        chunk = power(one, length)
        block_pow = power(chunk, CHUNKS)
        row = lax.broadcasted_iota(jnp.int32, (CHUNKS, width), 0)
        ahead = (jnp.ones((1, width), F32), jnp.zeros((1, width), F32))
        spread_re = jnp.zeros((CHUNKS, width), F32)
        spread_im = jnp.zeros((CHUNKS, width), F32)
        for s in range(CHUNKS):
            spread_re = jnp.where(row == s, ahead[0], spread_re)
            spread_im = jnp.where(row == s, ahead[1], spread_im)
            ahead = times(ahead, chunk)
        full = jnp.zeros((CHUNKS, width), F32)
        for slot, value in enumerate((*one, *chunk, *block_pow)):
            coef[i, slot] = full + value
        coef[i, 6] = spread_re
        coef[i, 7] = spread_im
    row = lax.broadcasted_iota(jnp.int32, (steps, steps), 0)
    col = lax.broadcasted_iota(jnp.int32, (steps, steps), 1)
    low, shift = CHUNKS - 1, CHUNKS.bit_length() - 1
    shuffle = (col == (row & low) * length + (row >> shift)).astype(BF16)
    restore[...] = (row == (col & low) * length + (col >> shift)).astype(BF16)

    for copy in wind_in:
        copy.wait_recv()
    v = lax.dot_general(shuffle, winds[...], (((1,), (1,)), ((), ())), preferred_element_type=F32)
    q = v * jnp.abs(v)
    q_hi = q.astype(BF16)
    q_lo = (q - q_hi.astype(F32)).astype(BF16)
    q2 = jnp.concatenate([q_hi, q_lo], axis=1)

    e_in = []
    sent_ends = []

    def first_pass(k):
        pr, px = plane(k, -1)
        group = pr * n_t + px
        if k:
            for copy in x_in[k]:
                copy.wait_recv()
        b = bases[group]
        forces[k] = jnp.dot(q2, jnp.concatenate([b, b], axis=0), preferred_element_type=F32)
        zr, zi = coef[group, 0], coef[group, 1]

        def step(j, state, k=k, zr=zr, zi=zi):
            f = forces[k, pl.ds(pl.multiple_of(j * CHUNKS, CHUNKS), CHUNKS), :]
            return (zr * state[0] - zi * state[1] + f, zr * state[1] + zi * state[0])

        zero = jnp.zeros((CHUNKS, width), F32)
        end_re, end_im = lax.fori_loop(0, length, step, (zero, zero), unroll=8)
        chunk = (coef[group, 2][:1], coef[group, 3][:1])
        row8 = lax.broadcasted_iota(jnp.int32, (CHUNKS, width), 0)
        state = (zero[:1], zero[:1])
        in_re, in_im = zero, zero
        for s in range(CHUNKS):
            if s:
                in_re = jnp.where(row8 == s, state[0], in_re)
                in_im = jnp.where(row8 == s, state[1], in_im)
            moved = times(chunk, state)
            state = (moved[0] + end_re[s : s + 1], moved[1] + end_im[s : s + 1])
        entry[k, 0] = in_re
        entry[k, 1] = in_im
        ends[x, group] = jnp.where(row8 == 0, state[0], state[1])
        arrivals = []
        for dx in range(1, n_t):
            block = ends.at[x, group]
            copy = remote(
                block, block, esend.at[group, dx - 1], erecv.at[group, dx - 1],
                {"tm": lax.rem(x + dx, n_t)},
            )
            pl.when(x + dx < n_t)(copy.start)
            sent_ends.append((dx, copy))
            arrivals.append((dx, copy))
        e_in.append(arrivals)

    def second_pass(k):
        pr, px = plane(k, -1)
        group = pr * n_t + px
        for dx, copy in e_in[k]:
            pl.when(x >= dx)(copy.wait_recv)
        cols = pl.ds(pl.multiple_of(group * width, width), width)
        prior = prior_ref[:, cols]
        state = (prior[:1], prior[1:2])
        block_pow = (coef[group, 4][:1], coef[group, 5][:1])
        for y in range(n_t - 1):
            moved = times(block_pow, state)
            e = ends[y, group]
            state = (
                jnp.where(y < x, moved[0] + e[:1], state[0]),
                jnp.where(y < x, moved[1] + e[1:2], state[1]),
            )
        start = times((coef[group, 6], coef[group, 7]), state)
        start = (start[0] + entry[k, 0], start[1] + entry[k, 1])
        zr, zi = coef[group, 0], coef[group, 1]

        def pair(j, state, k=k, zr=zr, zi=zi, cols=cols):
            imag = []
            f2 = forces[k, pl.ds(pl.multiple_of(j * 2 * CHUNKS, 2 * CHUNKS), 2 * CHUNKS), :]
            for s in range(2):
                f = f2[s * CHUNKS : (s + 1) * CHUNKS]
                state = (zr * state[0] - zi * state[1] + f, zr * state[1] + zi * state[0])
                imag.append(state[1])
            rows = pl.ds(pl.multiple_of(j * 2 * CHUNKS, 2 * CHUNKS), 2 * CHUNKS)
            resp[rows, cols] = jnp.concatenate(imag, axis=0).astype(BF16)
            return state

        lax.fori_loop(0, length // 2, pair, start, unroll=4)
        return cols

    theirs = pl.ds(pl.multiple_of((1 - c) * half, half), half)
    ours = pl.ds(pl.multiple_of(c * half, half), half)
    for k in range(groups):
        first_pass(k)
    load_rec.wait()
    turns = list(range(groups))
    for i, k in enumerate(turns[:-1]):
        cols = second_pass(k)
        product = jnp.dot(resp[:, cols], rec_v[cols, :], preferred_element_type=F32)
        if i:
            partial[...] += product
        else:
            partial[...] = product
    cols = second_pass(turns[-1])
    last = jnp.dot(resp[:, cols], rec_v[cols, theirs], preferred_element_type=F32)
    part_out[...] = (partial[:, theirs] + last).astype(BF16)
    swap = remote(part_out, part_in, rsend, rrecv, {"rep": 1 - c})
    swap.start()
    last = jnp.dot(resp[:, cols], rec_v[cols, ours], preferred_element_type=F32)
    own = partial[:, ours] + last
    swap.wait_recv()
    total = (own + part_in[...].astype(F32)).astype(BF16)
    out_ref[...] = jnp.dot(restore[...], total, preferred_element_type=F32).astype(BF16)
    swap.wait_send()
    for copy in pending:
        copy.wait_send()
    for dx, copy in sent_ends:
        pl.when(x + dx < n_t)(copy.wait_send)


def local(
    wind_speed, span_of_point, drag_factor, mode_shapes, damping, turning, prior_state, recovery
):
    n_r, n_z, n_t = (lax.axis_size(a) for a in ("runs", "pts", "tm"))
    groups = n_r * n_t
    spans, steps = wind_speed.shape
    points, modes = mode_shapes.shape
    clamps = recovery.shape[1]
    width = modes // groups
    pieces = n_z if n_z <= 4 else 1
    vmem = pl.BlockSpec(memory_space=pltpu.VMEM)
    hbm = pl.BlockSpec(memory_space=pltpu.HBM)
    dma = pltpu.SemaphoreType.DMA
    return pl.pallas_call(
        functools.partial(kernel, (n_r, n_z, n_t)),
        out_shape=jax.ShapeDtypeStruct((steps, clamps // 2), BF16),
        in_specs=[hbm] * 8,
        out_specs=vmem,
        scratch_shapes=[
            pltpu.VMEM((spans, steps), BF16),
            pltpu.VMEM((1, points), jnp.int32),
            pltpu.VMEM((1, points), F32),
            pltpu.VMEM((1, modes), F32),
            pltpu.VMEM((1, modes), F32),
            pltpu.VMEM((2, modes), F32),
            pltpu.VMEM((steps, steps), BF16),
            pltpu.VMEM((points, width), BF16),
            pltpu.VMEM((modes, clamps), BF16),
            pltpu.VMEM((n_z * spans, steps), BF16),
            pltpu.VMEM((groups, n_z * spans, width), BF16),
            pltpu.VMEM((groups, steps, width), F32),
            pltpu.VMEM((n_t, groups, CHUNKS, width), F32),
            pltpu.VMEM((groups, 2, CHUNKS, width), F32),
            pltpu.VMEM((groups, 8, CHUNKS, width), F32),
            pltpu.VMEM((steps, modes), BF16),
            pltpu.VMEM((steps, clamps), F32),
            pltpu.VMEM((steps, clamps // 2), BF16),
            pltpu.VMEM((steps, clamps // 2), BF16),
            dma((8,)),
            dma((n_z - 1,)),
            dma((n_z - 1,)),
            dma((n_z - 1,)),
            dma((n_z - 1,)),
            dma((groups - 1, pieces)),
            dma((groups - 1, pieces)),
            dma((groups, n_t - 1)),
            dma((groups, n_t - 1)),
            dma,
            dma,
        ],
        compiler_params=pltpu.CompilerParams(
            collective_id=0, has_side_effects=True, vmem_limit_bytes=64 * 1024 * 1024
        ),
    )(
        wind_speed,
        span_of_point.reshape(1, points),
        drag_factor.reshape(1, points),
        mode_shapes,
        damping.reshape(1, modes),
        turning.reshape(1, modes),
        prior_state,
        recovery,
    )


def solution(mesh):
    placed = (
        P(("runs", "pts"), "tm"),
        P("pts"),
        P("pts"),
        P("pts", "rep"),
        P("rep"),
        P("rep"),
        P("runs", "rep"),
        P("rep", "pts"),
    )
    return jax.shard_map(
        local,
        mesh=mesh,
        in_specs=placed,
        out_specs=P(("runs", "tm"), ("pts", "rep")),
        check_vma=False,
    )
```
